32 devices in a mesh: seq: 16 (over z, y, x), chan: 2 (over core).
Axes of the slice: x: 2, y: 2, z: 4, core: 2. Of those that a mesh axis runs over, the one named last changes fastest.
Arguments:
- signal: bfloat16 [2048, 2048], P('seq', 'chan'), may hold values from -6 to 6
- cotangent: bfloat16 [2048, 2048], P('seq', 'chan'), may hold values from -6 to 6
- w_proj: bfloat16 [2048, 560], P('chan'), may hold values from -0.013671875 to 0.013671875
- w_delta: bfloat16 [2, 256, 2048], P(None, None, 'chan'), may hold values from -3.5625 to 3.5625
- delta_bias: float32 [2, 2048], P(None, 'chan'), may hold values from -1 to 0.5
- decay_log: float32 [2, 12, 2048], P(None, None, 'chan'), may hold values from -12 to -3, as said below
- skip_gain: float32 [2048], P('chan'), may hold values from 0.5 to 1.5
Outputs:
- layer_out: bfloat16 [2048, 2048], P('seq', 'chan')
- signal_grad: bfloat16 [2048, 2048], P('seq', 'chan')
The draws below stay inside these ranges and needn't reach their ends.
Inputs may be any that keep to these rules, and one draw needn't show every extreme that they name: `decay_log`: each entry is the logarithm of a positive decay rate.
All inputs are finite; a program needn't handle non-finite values.
Results may differ from the reference program's by a relative error of at most 0.0085.
Values may be sent and summed in bfloat16 or wider, within the bound.
A program may use at most 64 MiB of HBM per device.

```python
import math
import jax
import jax.numpy as jnp
from jax import lax

D = 2048
STATE = 12
RANK = 256
TOKENS = 2048
PROJ = 560


def draw_decay_log(key, part):
    level_key, pick_key = jax.random.split(jax.random.fold_in(key, 11))
    level = jax.random.uniform(level_key, (2, STATE, D), jnp.float32)
    picker = jax.random.uniform(pick_key, (2, STATE, D), jnp.float32)
    slow_share = 0.5
    lowest = math.log(0.1 / TOKENS)
    middle = math.log(2.0 / TOKENS)
    highest = math.log(0.04)
    slow_part = lowest + level * (middle - lowest)
    fast_part = middle + level * (highest - middle)
    return jnp.where(picker < slow_share, slow_part, fast_part).astype(jnp.float32)


def level_of(rng, extent, cuts, low, high):
    level = 1.0
    for dim, shards_of in cuts:
        steps = jax.random.uniform(jax.random.fold_in(jax.random.fold_in(rng, 6), dim), (shards_of,), jnp.float32, low / len(cuts), high / len(cuts))
        level = level * jnp.repeat(jnp.exp(steps), extent[dim] // shards_of).reshape((-1,) + (1,) * (len(extent) - 1 - dim))
    return level


def gaussian(rng, shape, spread, most, cuts=(), held_as=jnp.bfloat16):
    factor_of = level_of(rng, shape, cuts, -0.22, 0.18) if cuts else 1.0
    result = jax.random.normal(rng, shape, jnp.float32) * spread * factor_of
    return jnp.minimum(jnp.maximum(result, -most), most).astype(held_as)


def setup_inputs(seed: int = 0) -> dict:
    streams_of = jax.random.split(jax.random.key(seed), 8)
    return {
        "signal": gaussian(streams_of[0], (TOKENS, D), 1.0, 6.0, ((0, 16), (1, 2))),
        "cotangent": gaussian(streams_of[1], (TOKENS, D), 1.0, 6.0, ((0, 16), (1, 2))),
        "w_proj": gaussian(streams_of[2], (D, PROJ), (D * 2 * TOKENS ** 0.5) ** -0.5, 0.013671875, ((0, 2),)),
        "w_delta": gaussian(streams_of[3], (2, RANK, D), ((2 * TOKENS ** 0.5 / RANK) ** 0.5), 3.5625, ((2, 2),)),
        "delta_bias": jnp.clip(-1.0 + 1.5 * jax.random.uniform(streams_of[4], (2, D), jnp.float32) ** level_of(streams_of[4], (2, D), ((1, 2),), -0.2, 0.2), -1.0, 0.5),
        "decay_log": draw_decay_log(jax.random.fold_in(streams_of[7], 71), 0),
        "skip_gain": jnp.clip(0.5 + 1.0 * jax.random.uniform(streams_of[6], (D,), jnp.float32) ** level_of(streams_of[6], (D,), ((0, 2),), -0.2, 0.2), 0.5, 1.5),
    }


def compose_one(earlier, later):
    return (earlier[0] * later[0], later[0] * earlier[1] + later[1])

def linear_scan(decay, drive, falling):
    return lax.associative_scan(compose_one, (decay, drive), reverse=falling, axis=0)[1]

def both_directions(signal_part, pre_fwd, pre_bwd, in_fwd, out_fwd, in_bwd, out_bwd, log_fwd, log_bwd):
    total = jnp.zeros(signal_part.shape, jnp.float32)
    for pre, in_mat, out_mat, logs, falling in ((pre_fwd, in_fwd, out_fwd, log_fwd, False), (pre_bwd, in_bwd, out_bwd, log_bwd, True)):
        delta = jax.nn.softplus(pre)
        rate = -jnp.exp(logs)
        decay = jnp.exp(delta[:, None, :] * rate[None])
        drive = (delta * signal_part)[:, None, :] * in_mat[:, :, None]
        states = linear_scan(decay, drive, falling)
        total = total + lax.optimization_barrier(jnp.sum(out_mat[:, :, None] * states, 1))
    return total

def reference(signal, cotangent, w_proj, w_delta, delta_bias, decay_log, skip_gain):
    projected = jnp.dot(signal, w_proj, preferred_element_type=jnp.float32).astype(jnp.bfloat16)
    low_fwd = projected[:, :RANK]
    low_bwd = projected[:, RANK:2 * RANK]
    gates = projected[:, 2 * RANK:].astype(jnp.float32)
    in_fwd = gates[:, :STATE]
    out_fwd = gates[:, STATE:2 * STATE]
    in_bwd = gates[:, 2 * STATE:3 * STATE]
    out_bwd = gates[:, 3 * STATE:4 * STATE]
    pre_fwd = jnp.dot(low_fwd, w_delta[0], preferred_element_type=jnp.float32) + delta_bias[0]
    pre_bwd = jnp.dot(low_bwd, w_delta[1], preferred_element_type=jnp.float32) + delta_bias[1]
    signal_wide = signal.astype(jnp.float32)
    cot_wide = cotangent.astype(jnp.float32)
    lanes = min(128, D)
    blocks = D // lanes

    def split(array):
        return array.reshape(TOKENS, blocks, lanes).transpose(1, 0, 2)

    def join(array):
        return array.transpose(1, 0, 2).reshape(TOKENS, D)
    log_blocks = decay_log.reshape(2, STATE, blocks, lanes).transpose(2, 0, 1, 3)

    def per_block(items):
        signal_part, pre_one, pre_two, cot_part, logs = items

        def core_fn(sig_in, first_pre, second_pre, in_one, out_one, in_two, out_two):
            return both_directions(sig_in, first_pre, second_pre, in_one, out_one, in_two, out_two, logs[0], logs[1])
        core_part, pullback = jax.vjp(core_fn, signal_part, pre_one, pre_two, in_fwd, out_fwd, in_bwd, out_bwd)
        return (core_part,) + tuple(pullback(cot_part))
    results = lax.map(per_block, (split(signal_wide), split(pre_fwd), split(pre_bwd), split(cot_wide), log_blocks))
    core = join(results[0])
    grad_sig = join(results[1])
    grad_pre_fwd = join(results[2]).astype(jnp.bfloat16)
    grad_pre_bwd = join(results[3]).astype(jnp.bfloat16)
    grad_in_fwd = lax.optimization_barrier(jnp.sum(results[4], 0))
    grad_out_fwd = lax.optimization_barrier(jnp.sum(results[5], 0))
    grad_in_bwd = lax.optimization_barrier(jnp.sum(results[6], 0))
    grad_out_bwd = lax.optimization_barrier(jnp.sum(results[7], 0))
    layer_out = (core + skip_gain * signal_wide).astype(jnp.bfloat16)
    dims = (((1,), (1,)), ((), ()))
    grad_low_fwd = lax.dot_general(grad_pre_fwd, w_delta[0], dims, preferred_element_type=jnp.float32)
    grad_low_bwd = lax.dot_general(grad_pre_bwd, w_delta[1], dims, preferred_element_type=jnp.float32)
    grad_proj = jnp.concatenate([grad_low_fwd, grad_low_bwd, grad_in_fwd, grad_out_fwd, grad_in_bwd, grad_out_bwd], 1).astype(jnp.bfloat16)
    signal_grad = lax.dot_general(grad_proj, w_proj, dims, preferred_element_type=jnp.float32) + grad_sig + skip_gain * cot_wide
    return (layer_out, signal_grad.astype(jnp.bfloat16))
```

```python
import functools
import math

import jax
import jax.numpy as jnp
from jax import lax
from jax.experimental import pallas as pl
from jax.experimental.pallas import tpu as pltpu
from jax.sharding import PartitionSpec as P

SUB = 8
LANES = 128
LIMIT = 56 * 1024 * 1024
F32 = jnp.float32
BF16 = jnp.bfloat16
LOG2E = math.log2(math.e)
NT = (((1,), (1,)), ((), ()))


def mm(a, b):
    return jnp.dot(a, b, preferred_element_type=F32)


def order_matrix(rows, back):
    steps = rows // SUB
    work, token = (1, 0) if back else (0, 1)
    r = lax.broadcasted_iota(jnp.int32, (rows, rows), work)
    t = lax.broadcasted_iota(jnp.int32, (rows, rows), token)
    return jnp.where(t == (r & (SUB - 1)) * steps + (r >> 3), 1.0, 0.0).astype(BF16)


def tile_rows(step):
    return pl.ds(pl.multiple_of(step * SUB, SUB), SUB)


def tile_cols(block):
    return pl.ds(pl.multiple_of(block * LANES, LANES), LANES)


def softplus(x):
    return jnp.maximum(x, 0.0) + jnp.log1p(jnp.exp(-jnp.abs(x)))


def fill_rates(log_ref, rate_ref):
    depth = log_ref.shape[1]
    for k in range(2):
        rate = jnp.exp(log_ref[k]) * (-LOG2E)
        for n in range(depth):
            rate_ref[k * depth + n] = jnp.broadcast_to(rate[n : n + 1], rate_ref.shape[1:])


def fill_gates(gates, gate_ref):
    for m in range(gate_ref.shape[0]):
        gate_ref[m] = jnp.broadcast_to(gates[:, m : m + 1], gate_ref.shape[1:])


def project_kernel(sig_ref, cot_ref, w_ref, part_ref, sigp_ref, cotp_ref):
    order = order_matrix(sig_ref.shape[0], False)
    sig = mm(order, sig_ref[...]).astype(BF16)
    sigp_ref[...] = sig
    cotp_ref[...] = mm(order, cot_ref[...]).astype(BF16)
    part_ref[...] = mm(sig, w_ref[...])


def sublane_scan(decay, value, rising):
    sub = lax.broadcasted_iota(jnp.int32, value.shape, 0)
    shift = 1
    while shift < SUB:
        amount = shift if rising else SUB - shift
        has = (sub >= shift) if rising else (sub < SUB - shift)
        value = value + decay * jnp.where(has, pltpu.roll(value, amount, 0), 0.0)
        decay = decay * jnp.where(has, pltpu.roll(decay, amount, 0), 1.0)
        shift *= 2
    edge = (sub >= 1) if rising else (sub < SUB - 1)
    before = jnp.where(edge, pltpu.roll(value, 1 if rising else SUB - 1, 0), 0.0)
    last = SUB - 1 if rising else 0
    return before, value[last : last + 1]


def summary_kernel(
    proj_ref, sigp_ref, cotp_ref, wd_ref, bias_ref, log_ref,
    pre_ref, entry_ref, span_ref, dev_ref, total_ref,
    delta_ref, sig_ref, cot_ref, gate_ref, rate_ref, edge_ref,
):
    rows, width = sigp_ref.shape
    depth = log_ref.shape[1]
    rank = wd_ref.shape[1]
    steps = rows // SUB
    proj = proj_ref[...]
    for k in range(2):
        pre = mm(proj[:, k * rank : (k + 1) * rank], wd_ref[k]) + bias_ref[k : k + 1, :]
        pre_ref[k] = pre
        delta_ref[k] = softplus(pre)
    sig_ref[...] = sigp_ref[...].astype(F32)
    cot_ref[...] = cotp_ref[...].astype(F32)
    fill_gates(proj[:, 2 * rank :].astype(F32), gate_ref)
    fill_rates(log_ref, rate_ref)
    half = (depth + 1) // 2

    def block_body(block, _):
        cols = tile_cols(block)
        zero = jnp.zeros((SUB, LANES), F32)
        for k in range(2):
            for first in range(0, depth, half):
                ns = range(first, min(first + half, depth))

                def step_body(i, carry, ns=ns, k=k):
                    span, state, power, adjoint = carry
                    for u in range(2):
                        at = i * 2 + u
                        here = tile_rows(at if k == 0 else steps - 1 - at)
                        delta = delta_ref[k, here, cols]
                        weight = delta * sig_ref[here, cols]
                        cot = cot_ref[here, cols]
                        span = span + delta
                        new = ([], [], [])
                        for j, n in enumerate(ns):
                            a = jnp.exp2(delta * rate_ref[k * depth + n, :, cols])
                            p = a * power[j]
                            new[0].append(
                                a * state[j] + weight * gate_ref[2 * k * depth + n, here, :]
                            )
                            new[1].append(p)
                            new[2].append(
                                adjoint[j] + p * (cot * gate_ref[(2 * k + 1) * depth + n, here, :])
                            )
                        state, power, adjoint = (tuple(x) for x in new)
                    return span, state, power, adjoint

                zeros = (zero,) * len(ns)
                ones = (jnp.ones((SUB, LANES), F32),) * len(ns)
                span, state, power, adjoint = lax.fori_loop(
                    0, steps // 2, step_body, (zero, zeros, ones, zeros)
                )
                if first == 0:
                    one = jnp.ones((SUB, LANES), F32)
                    below, whole = sublane_scan(one, span, True)
                    above, _unused = sublane_scan(one, span, False)
                    span_ref[0, k, :, cols] = below
                    span_ref[1, k, :, cols] = above
                    total_ref[k : k + 1, cols] = whole
                for j, n in enumerate(ns):
                    row = k * depth + n
                    for kind, value in ((0, state[j]), (1, adjoint[j])):
                        group = k ^ kind
                        before, edge = sublane_scan(power[j], value, group == 0)
                        entry_ref[group, row, :, cols] = before
                        edge_ref[group, row : row + 1, cols] = edge
        return 0

    lax.fori_loop(0, width // LANES, block_body, 0)
    dev_ref[...] = edge_ref[...].astype(BF16)


def scan_kernel(
    pos_ref, proj_ref, sigp_ref, cotp_ref, pre_ref, wd_ref, log_ref, skip_ref,
    entry_ref, span_ref, devs_ref, totals_ref,
    out_ref, part_ref, base_ref,
    delta_ref, sig_ref, cot_ref, gate_ref, rate_ref, enter_ref,
    core_ref, gsig_ref, gpre_ref, acc_ref, keep_ref, decay_ref,
):
    rows, width = sigp_ref.shape
    depth = log_ref.shape[1]
    rank = wd_ref.shape[1]
    steps = rows // SUB
    peers = devs_ref.shape[0]
    position = pos_ref[0]
    for k in range(2):
        delta_ref[k] = softplus(pre_ref[k])
    sig_ref[...] = sigp_ref[...].astype(F32)
    cot_ref[...] = cotp_ref[...].astype(F32)
    fill_gates(proj_ref[:, 2 * rank :].astype(F32), gate_ref)
    fill_rates(log_ref, rate_ref)
    acc_ref[...] = jnp.zeros_like(acc_ref)
    core_ref[...] = jnp.zeros_like(core_ref)
    gsig_ref[...] = jnp.zeros_like(gsig_ref)

    rates = jnp.concatenate([log_ref[0], log_ref[1]], 0)
    rates = jnp.exp(rates) * (-LOG2E)
    upper = lax.broadcasted_iota(jnp.int32, rates.shape, 0) < depth
    for group in range(2):
        enter_ref[group] = jnp.zeros(rates.shape, F32)

        def join(j, _, group=group):
            peer = j if group == 0 else peers - 1 - j
            use = (peer < position) if group == 0 else (peer > position)

            @pl.when(use)
            def _():
                total = totals_ref[peer]
                wide = jnp.where(upper, total[0:1], total[1:2])
                enter_ref[group] = enter_ref[group] * jnp.exp2(rates * wide) + devs_ref[
                    peer, group
                ].astype(F32)

            return 0

        lax.fori_loop(0, peers, join, 0)

    def start(group, k, n, cols):
        row = k * depth + n
        decay = jnp.exp2(rate_ref[row, :, cols] * span_ref[group, k, :, cols])
        return entry_ref[group, row, :, cols] + decay * enter_ref[group, row : row + 1, cols]

    def block_body(block, _):
        cols = tile_cols(block)
        for k in range(2):
            gate_in = 2 * k * depth
            gate_out = gate_in + depth

            def forward(i, states, k=k, gate_in=gate_in, gate_out=gate_out):
                for u in range(2):
                    at = i * 2 + u
                    at = at if k == 0 else steps - 1 - at
                    here = tile_rows(at)
                    delta = delta_ref[k, here, cols]
                    weight = delta * sig_ref[here, cols]
                    cot = cot_ref[here, cols]
                    core = core_ref[here, cols]
                    new = []
                    for n in range(depth):
                        a = jnp.exp2(delta * rate_ref[k * depth + n, :, cols])
                        kept = a * states[n]
                        h = kept + weight * gate_ref[gate_in + n, here, :]
                        decay_ref[at, n] = a
                        keep_ref[at, n] = kept
                        core = core + gate_ref[gate_out + n, here, :] * h
                        lane = slice((gate_out + n) * LANES, (gate_out + n + 1) * LANES)
                        acc_ref[here, lane] += cot * h
                        new.append(h)
                    core_ref[here, cols] = core
                    states = tuple(new)
                return states

            lax.fori_loop(
                0, steps // 2, forward, tuple(start(k, k, n, cols) for n in range(depth))
            )

            def backward(i, carried, k=k, gate_in=gate_in, gate_out=gate_out):
                for u in range(2):
                    at = i * 2 + u
                    at = steps - 1 - at if k == 0 else at
                    here = tile_rows(at)
                    delta = delta_ref[k, here, cols]
                    sig = sig_ref[here, cols]
                    weight = delta * sig
                    cot = cot_ref[here, cols]
                    by_in = jnp.zeros((SUB, LANES), F32)
                    by_decay = jnp.zeros((SUB, LANES), F32)
                    new = []
                    for n in range(depth):
                        adjoint = cot * gate_ref[gate_out + n, here, :] + carried[n]
                        by_in = by_in + adjoint * gate_ref[gate_in + n, here, :]
                        by_decay = by_decay + adjoint * (
                            keep_ref[at, n] * rate_ref[k * depth + n, :, cols]
                        )
                        lane = slice((gate_in + n) * LANES, (gate_in + n + 1) * LANES)
                        acc_ref[here, lane] += adjoint * weight
                        new.append(decay_ref[at, n] * adjoint)
                    gsig_ref[here, cols] += by_in * delta
                    gpre_ref[k, here, cols] = by_in * sig + by_decay * (1.0 / LOG2E)
                    carried = tuple(new)
                return carried

            lax.fori_loop(
                0, steps // 2, backward, tuple(start(1 - k, k, n, cols) for n in range(depth))
            )
        return 0

    lax.fori_loop(0, width // LANES, block_body, 0)

    skip = skip_ref[...]
    layer = (core_ref[...] + skip * sig_ref[...]).astype(BF16)
    out_ref[...] = mm(order_matrix(rows, True), layer).astype(BF16)
    base_ref[...] = gsig_ref[...] + skip * cot_ref[...]
    for k in range(2):
        slope = 1.0 / (1.0 + jnp.exp(-pre_ref[k]))
        grad_pre = (gpre_ref[k] * slope).astype(BF16)
        part_ref[:, k * rank : (k + 1) * rank] = lax.dot_general(
            grad_pre, wd_ref[k], NT, preferred_element_type=F32
        )
    gates = 4 * depth
    acc = acc_ref[...]
    high = acc.astype(BF16)
    low = (acc - high.astype(F32)).astype(BF16)
    lane = lax.broadcasted_iota(jnp.int32, (gates * LANES, gates), 0) >> 7
    column = lax.broadcasted_iota(jnp.int32, (gates * LANES, gates), 1)
    ones = jnp.where(lane == column, 1.0, 0.0).astype(BF16)
    part_ref[:, 2 * rank :] = mm(high, ones) + mm(low, ones)


def final_kernel(gproj_ref, w_ref, base_ref, out_ref):
    rows = out_ref.shape[0]
    grad = lax.dot_general(gproj_ref[...], w_ref[...], NT, preferred_element_type=F32)
    grad = (grad + base_ref[...]).astype(BF16)
    out_ref[...] = mm(order_matrix(rows, True), grad).astype(BF16)


def shape(dims, dtype=F32):
    return jax.ShapeDtypeStruct(dims, dtype)


def call(kernel, out_shape, scratch, smem=0):
    def run(*args):
        specs = [
            pl.BlockSpec(memory_space=pltpu.SMEM if i < smem else pltpu.VMEM)
            for i in range(len(args))
        ]
        return pl.pallas_call(
            kernel,
            out_shape=out_shape,
            in_specs=specs,
            out_specs=jax.tree.map(lambda _: pl.BlockSpec(memory_space=pltpu.VMEM), out_shape),
            scratch_shapes=scratch,
            compiler_params=pltpu.CompilerParams(vmem_limit_bytes=LIMIT),
        )(*args)

    return run


def local(signal, cotangent, w_proj, w_delta, delta_bias, decay_log, skip_gain):
    rows, width = signal.shape
    rank = w_delta.shape[1]
    depth = decay_log.shape[1]
    steps = rows // SUB
    proj = w_proj.shape[1]
    gates = 4 * depth
    vmem = lambda *dims: pltpu.VMEM(dims, F32)
    part, sigp, cotp = call(
        project_kernel,
        (shape((rows, proj)), shape((rows, width), BF16), shape((rows, width), BF16)),
        [],
    )(signal, cotangent, w_proj)
    projected = lax.psum(part, "chan").astype(BF16)
    common = [
        vmem(2, rows, width),
        vmem(rows, width),
        vmem(rows, width),
        vmem(gates, rows, LANES),
        vmem(2 * depth, SUB, width),
        vmem(2, 2 * depth, width),
    ]
    pre, entry, span, dev, total = call(
        summary_kernel,
        (
            shape((2, rows, width)),
            shape((2, 2 * depth, SUB, width)),
            shape((2, 2, SUB, width)),
            shape((2, 2 * depth, width), BF16),
            shape((2, width)),
        ),
        common,
    )(projected, sigp, cotp, w_delta, delta_bias, decay_log)
    devs = lax.all_gather(dev, "seq", axis=0)
    totals = lax.all_gather(total, "seq", axis=0)
    position = lax.axis_index("seq").astype(jnp.int32).reshape(1)
    layer_out, grad_part, base = call(
        scan_kernel,
        (shape((rows, width), BF16), shape((rows, proj)), shape((rows, width))),
        common
        + [
            vmem(rows, width),
            vmem(rows, width),
            vmem(2, rows, width),
            vmem(rows, gates * LANES),
            vmem(steps, depth, SUB, LANES),
            vmem(steps, depth, SUB, LANES),
        ],
        smem=1,
    )(
        position, projected, sigp, cotp, pre, w_delta, decay_log, skip_gain.reshape(1, width),
        entry, span, devs, totals,
    )
    grad_proj = lax.psum(grad_part, "chan").astype(BF16)
    signal_grad = call(final_kernel, shape((rows, width), BF16), [])(grad_proj, w_proj, base)
    return (layer_out, signal_grad)


def solution(mesh):
    in_specs = (
        P("seq", "chan"),
        P("seq", "chan"),
        P("chan", None),
        P(None, None, "chan"),
        P(None, "chan"),
        P(None, None, "chan"),
        P("chan"),
    )
    out_specs = (P("seq", "chan"), P("seq", "chan"))
    return jax.shard_map(local, mesh=mesh, in_specs=in_specs, out_specs=out_specs, check_vma=False)
```

```python
import functools
import math

import jax
import jax.numpy as jnp
from jax import lax
from jax.experimental import pallas as pl
from jax.experimental.pallas import tpu as pltpu
from jax.sharding import PartitionSpec as P

SUB = 8
LANES = 128
MESH = pl.DeviceIdType.MESH
LIMIT = 56 * 1024 * 1024
F32 = jnp.float32
BF16 = jnp.bfloat16
LOG2E = math.log2(math.e)
NT = (((1,), (1,)), ((), ()))


def mm(a, b):
    return jnp.dot(a, b, preferred_element_type=F32)


def order_matrix(rows, back):
    steps = rows // SUB
    work, token = (1, 0) if back else (0, 1)
    r = lax.broadcasted_iota(jnp.int32, (rows, rows), work)
    t = lax.broadcasted_iota(jnp.int32, (rows, rows), token)
    return jnp.where(t == (r & (SUB - 1)) * steps + (r >> 3), 1.0, 0.0).astype(BF16)


def tile_rows(step):
    return pl.ds(pl.multiple_of(step * SUB, SUB), SUB)


def tile_cols(block):
    return pl.ds(pl.multiple_of(block * LANES, LANES), LANES)


def softplus(x):
    return jnp.maximum(x, 0.0) + jnp.log1p(jnp.exp(-jnp.abs(x)))


def fill_rates(log_ref, rate_ref):
    depth = log_ref.shape[0]
    for k in range(2):
        rate = jnp.exp(log_ref[:, k]) * (-LOG2E)
        for n in range(depth):
            rate_ref[k * depth + n] = jnp.broadcast_to(rate[n : n + 1], rate_ref.shape[1:])


def fill_gates(gates, gate_ref):
    for m in range(gate_ref.shape[0]):
        gate_ref[m] = jnp.broadcast_to(gates[:, m : m + 1], gate_ref.shape[1:])


def greet(places):
    barrier = pltpu.get_barrier_semaphore()
    for place in places:
        pl.semaphore_signal(barrier, inc=1, device_id=place, device_id_type=MESH)
    return barrier, len(places)


def share_and_sum(peers, slots_ref, send_sem, recv_sem, greeting):
    me = lax.axis_index("chan")
    pl.semaphore_wait(*greeting)
    sends = []
    for o in range(1, peers):
        copy = pltpu.make_async_remote_copy(
            src_ref=slots_ref.at[me],
            dst_ref=slots_ref.at[me],
            send_sem=send_sem.at[o - 1],
            recv_sem=recv_sem.at[o - 1],
            device_id={"chan": lax.rem(me + o, peers)},
            device_id_type=MESH,
        )
        copy.start()
        sends.append(copy)
    for o in range(1, peers):
        origin = lax.rem(me + peers - o, peers)
        pltpu.make_async_remote_copy(
            src_ref=slots_ref.at[origin],
            dst_ref=slots_ref.at[origin],
            send_sem=send_sem.at[o - 1],
            recv_sem=recv_sem.at[o - 1],
            device_id={"chan": origin},
            device_id_type=MESH,
        ).wait_recv()
    total = slots_ref[0]
    for p in range(1, peers):
        total = total + slots_ref[p]
    return total, sends


def chan_places(peers):
    me = lax.axis_index("chan")
    return [{"chan": lax.rem(me + o, peers)} for o in range(1, peers)]


def project_kernel(
    peers, sig_ref, cot_ref, w_ref, proj_ref, sigp_ref, cotp_ref, slots_ref, send_sem, recv_sem
):
    greeting = greet(chan_places(peers))
    me = lax.axis_index("chan")
    order = order_matrix(sig_ref.shape[0], False)
    sig = mm(order, sig_ref[...]).astype(BF16)
    slots_ref[me] = lax.dot_general(sig, w_ref[...], NT, preferred_element_type=F32)
    sigp_ref[...] = sig
    cotp_ref[...] = mm(order, cot_ref[...]).astype(BF16)
    total, sends = share_and_sum(peers, slots_ref, send_sem, recv_sem, greeting)
    proj_ref[...] = total.astype(BF16)
    for copy in sends:
        copy.wait_send()


def radices(count):
    found = []
    while count % 4 == 0 and count > 4:
        small = count % 16 == 0 and not found
        found += [2, 2] if small else [4]
        count //= 4
    return found + ([count] if count > 1 else [])


def place_at(me, stride, radix, shift):
    digit = lax.rem(me // stride, radix)
    return me + (lax.rem(digit + shift, radix) - digit) * stride


def exchange_kernel(
    levels, log_ref, dev_ref, total_ref, enter_ref,
    part_refs, span_refs, run_ref, wide_ref, send_sem, recv_sem,
):
    me = lax.axis_index("seq")
    depth = log_ref.shape[0]
    places = []
    stride = 1
    for radix in levels:
        places += [{"seq": place_at(me, stride, radix, o)} for o in range(1, radix)]
        stride *= radix
    greeting = greet(places)
    rates = jnp.concatenate([log_ref[:, 0], log_ref[:, 1]], 0)
    rates = jnp.exp(rates) * (-LOG2E)
    upper = lax.broadcasted_iota(jnp.int32, rates.shape, 0) < depth

    def power(span):
        return jnp.exp2(rates * jnp.where(upper, span[0:1], span[1:2]))

    enter_ref[...] = jnp.zeros_like(enter_ref)
    wide_ref[...] = jnp.zeros_like(wide_ref)
    pl.semaphore_wait(*greeting)
    stride = 1
    base = 0
    sends = []
    for level, radix in enumerate(levels):
        last = level == len(levels) - 1
        digit = lax.rem(me // stride, radix)
        parts, spans = part_refs[level], span_refs[level]
        if level == 0:
            parts[digit] = dev_ref[...]
            spans[digit] = total_ref[...]

        def copies(slot, place, o, group):
            at = base + 2 * (o - 1)
            block = parts.at[slot, group] if last else parts.at[slot]
            return [
                pltpu.make_async_remote_copy(
                    src_ref=ref,
                    dst_ref=ref,
                    send_sem=send_sem.at[at + i],
                    recv_sem=recv_sem.at[at + i],
                    device_id={"seq": place},
                    device_id_type=MESH,
                )
                for i, ref in enumerate((block, spans.at[slot]))
            ]

        for o in range(1, radix):
            peer = lax.rem(digit + o, radix)
            group = jnp.where(peer > digit, 0, 1)
            for copy in copies(digit, place_at(me, stride, radix, o), o, group):
                copy.start()
                sends.append(copy)
        for o in range(1, radix):
            peer = lax.rem(digit + radix - o, radix)
            group = jnp.where(peer < digit, 0, 1)
            for copy in copies(peer, place_at(me, stride, radix, radix - o), o, group):
                copy.wait_recv()

        for group in range(2):
            run_ref[...] = jnp.zeros_like(run_ref)
            far = jnp.zeros(total_ref.shape, F32)
            old = power(wide_ref[group])
            for step in range(radix):
                d = step if group == 0 else radix - 1 - step
                mine = digit == d

                @pl.when(mine)
                def _(group=group, far=far, old=old):
                    enter_ref[group] = enter_ref[group] + old * run_ref[...]
                    wide_ref[group] = wide_ref[group] + far

                ahead = (digit > d) if group == 0 else (digit < d)
                if last:

                    @pl.when(ahead)
                    def _(d=d, group=group):
                        run_ref[...] = run_ref[...] * power(spans[d]) + parts[d, group].astype(F32)

                else:
                    run_ref[...] = run_ref[...] * power(spans[d]) + parts[d, group].astype(F32)
                    far = far + spans[d]
            if not last:
                following = lax.rem(me // (stride * radix), levels[level + 1])
                part_refs[level + 1][following, group] = run_ref[...].astype(BF16)
                if group == 0:
                    span_refs[level + 1][following] = far
        base += 2 * (radix - 1)
        stride *= radix
    for copy in sends:
        copy.wait_send()


def sublane_scan(decay, value, rising):
    sub = lax.broadcasted_iota(jnp.int32, value.shape, 0)
    shift = 1
    while shift < SUB:
        amount = shift if rising else SUB - shift
        has = (sub >= shift) if rising else (sub < SUB - shift)
        value = value + decay * jnp.where(has, pltpu.roll(value, amount, 0), 0.0)
        decay = decay * jnp.where(has, pltpu.roll(decay, amount, 0), 1.0)
        shift *= 2
    edge = (sub >= 1) if rising else (sub < SUB - 1)
    before = jnp.where(edge, pltpu.roll(value, 1 if rising else SUB - 1, 0), 0.0)
    last = SUB - 1 if rising else 0
    return before, value[last : last + 1]


def summary_kernel(
    proj_ref, sigp_ref, cotp_ref, wd_ref, bias_ref, log_ref,
    pre_ref, entry_ref, span_ref, dev_ref, total_ref,
    delta_ref, sig_ref, cot_ref, gate_ref, rate_ref, edge_ref,
):
    rows, width = sigp_ref.shape
    depth = log_ref.shape[0]
    rank = wd_ref.shape[1]
    steps = rows // SUB
    proj = proj_ref[...]
    for k in range(2):
        pre = mm(proj[:, k * rank : (k + 1) * rank], wd_ref[k]) + bias_ref[k : k + 1, :]
        pre_ref[k] = pre
        delta_ref[k] = softplus(pre)
    sig_ref[...] = sigp_ref[...].astype(F32)
    cot_ref[...] = cotp_ref[...].astype(F32)
    fill_gates(proj[:, 2 * rank :].astype(F32), gate_ref)
    fill_rates(log_ref, rate_ref)
    half = (depth + 1) // 2

    def block_body(block, _):
        cols = tile_cols(block)
        zero = jnp.zeros((SUB, LANES), F32)
        for k in range(2):
            for first in range(0, depth, half):
                ns = range(first, min(first + half, depth))

                def step_body(i, carry, ns=ns, k=k):
                    span, state, power, adjoint = carry
                    for u in range(2):
                        at = i * 2 + u
                        here = tile_rows(at if k == 0 else steps - 1 - at)
                        delta = delta_ref[k, here, cols]
                        weight = delta * sig_ref[here, cols]
                        cot = cot_ref[here, cols]
                        span = span + delta
                        new = ([], [], [])
                        for j, n in enumerate(ns):
                            a = jnp.exp2(delta * rate_ref[k * depth + n, :, cols])
                            p = a * power[j]
                            new[0].append(
                                a * state[j] + weight * gate_ref[2 * k * depth + n, here, :]
                            )
                            new[1].append(p)
                            new[2].append(
                                adjoint[j] + p * (cot * gate_ref[(2 * k + 1) * depth + n, here, :])
                            )
                        state, power, adjoint = (tuple(x) for x in new)
                    return span, state, power, adjoint

                zeros = (zero,) * len(ns)
                ones = (jnp.ones((SUB, LANES), F32),) * len(ns)
                span, state, power, adjoint = lax.fori_loop(
                    0, steps // 2, step_body, (zero, zeros, ones, zeros)
                )
                if first == 0:
                    one = jnp.ones((SUB, LANES), F32)
                    below, whole = sublane_scan(one, span, True)
                    above, _unused = sublane_scan(one, span, False)
                    span_ref[0, k, :, cols] = below
                    span_ref[1, k, :, cols] = above
                    total_ref[k : k + 1, cols] = whole
                for j, n in enumerate(ns):
                    row = k * depth + n
                    for kind, value in ((0, state[j]), (1, adjoint[j])):
                        group = k ^ kind
                        before, edge = sublane_scan(power[j], value, group == 0)
                        entry_ref[group, row, :, cols] = before
                        edge_ref[group, row : row + 1, cols] = edge
        return 0

    lax.fori_loop(0, width // LANES, block_body, 0)
    dev_ref[...] = edge_ref[...].astype(BF16)


def scan_kernel(
    proj_ref, sigp_ref, cotp_ref, pre_ref, wd_ref, log_ref, skip_ref,
    entry_ref, span_ref, enter_ref,
    out_ref, part_ref, base_ref,
    delta_ref, sig_ref, cot_ref, gate_ref, rate_ref,
    core_ref, gsig_ref, gpre_ref, acc_ref, keep_ref, decay_ref,
):
    rows, width = sigp_ref.shape
    depth = log_ref.shape[0]
    rank = wd_ref.shape[1]
    steps = rows // SUB
    for k in range(2):
        delta_ref[k] = softplus(pre_ref[k])
    sig_ref[...] = sigp_ref[...].astype(F32)
    cot_ref[...] = cotp_ref[...].astype(F32)
    fill_gates(proj_ref[:, 2 * rank :].astype(F32), gate_ref)
    fill_rates(log_ref, rate_ref)
    acc_ref[...] = jnp.zeros_like(acc_ref)
    core_ref[...] = jnp.zeros_like(core_ref)
    gsig_ref[...] = jnp.zeros_like(gsig_ref)

    def start(group, k, n, cols):
        row = k * depth + n
        decay = jnp.exp2(rate_ref[row, :, cols] * span_ref[group, k, :, cols])
        return entry_ref[group, row, :, cols] + decay * enter_ref[group, row : row + 1, cols]

    def block_body(block, _):
        cols = tile_cols(block)
        for k in range(2):
            gate_in = 2 * k * depth
            gate_out = gate_in + depth

            def forward(i, states, k=k, gate_in=gate_in, gate_out=gate_out):
                for u in range(2):
                    at = i * 2 + u
                    at = at if k == 0 else steps - 1 - at
                    here = tile_rows(at)
                    delta = delta_ref[k, here, cols]
                    weight = delta * sig_ref[here, cols]
                    cot = cot_ref[here, cols]
                    core = core_ref[here, cols]
                    new = []
                    for n in range(depth):
                        a = jnp.exp2(delta * rate_ref[k * depth + n, :, cols])
                        kept = a * states[n]
                        h = kept + weight * gate_ref[gate_in + n, here, :]
                        decay_ref[at, n] = a
                        keep_ref[at, n] = kept
                        core = core + gate_ref[gate_out + n, here, :] * h
                        lane = slice((gate_out + n) * LANES, (gate_out + n + 1) * LANES)
                        acc_ref[here, lane] += cot * h
                        new.append(h)
                    core_ref[here, cols] = core
                    states = tuple(new)
                return states

            lax.fori_loop(
                0, steps // 2, forward, tuple(start(k, k, n, cols) for n in range(depth))
            )

            def backward(i, carried, k=k, gate_in=gate_in, gate_out=gate_out):
                for u in range(2):
                    at = i * 2 + u
                    at = steps - 1 - at if k == 0 else at
                    here = tile_rows(at)
                    delta = delta_ref[k, here, cols]
                    sig = sig_ref[here, cols]
                    weight = delta * sig
                    cot = cot_ref[here, cols]
                    by_in = jnp.zeros((SUB, LANES), F32)
                    by_decay = jnp.zeros((SUB, LANES), F32)
                    new = []
                    for n in range(depth):
                        adjoint = cot * gate_ref[gate_out + n, here, :] + carried[n]
                        by_in = by_in + adjoint * gate_ref[gate_in + n, here, :]
                        by_decay = by_decay + adjoint * (
                            keep_ref[at, n] * rate_ref[k * depth + n, :, cols]
                        )
                        lane = slice((gate_in + n) * LANES, (gate_in + n + 1) * LANES)
                        acc_ref[here, lane] += adjoint * weight
                        new.append(decay_ref[at, n] * adjoint)
                    gsig_ref[here, cols] += by_in * delta
                    gpre_ref[k, here, cols] = by_in * sig + by_decay * (1.0 / LOG2E)
                    carried = tuple(new)
                return carried

            lax.fori_loop(
                0, steps // 2, backward, tuple(start(1 - k, k, n, cols) for n in range(depth))
            )
        return 0

    lax.fori_loop(0, width // LANES, block_body, 0)

    skip = skip_ref[...]
    layer = (core_ref[...] + skip * sig_ref[...]).astype(BF16)
    out_ref[...] = mm(order_matrix(rows, True), layer).astype(BF16)
    base_ref[...] = gsig_ref[...] + skip * cot_ref[...]
    for k in range(2):
        slope = 1.0 / (1.0 + jnp.exp(-pre_ref[k]))
        grad_pre = (gpre_ref[k] * slope).astype(BF16)
        part_ref[:, k * rank : (k + 1) * rank] = lax.dot_general(
            grad_pre, wd_ref[k], NT, preferred_element_type=F32
        )
    gates = 4 * depth
    acc = acc_ref[...]
    high = acc.astype(BF16)
    low = (acc - high.astype(F32)).astype(BF16)
    lane = lax.broadcasted_iota(jnp.int32, (gates * LANES, gates), 0) >> 7
    column = lax.broadcasted_iota(jnp.int32, (gates * LANES, gates), 1)
    ones = jnp.where(lane == column, 1.0, 0.0).astype(BF16)
    part_ref[:, 2 * rank :] = mm(high, ones) + mm(low, ones)


def final_kernel(
    peers, part_ref, w_ref, base_ref, out_ref, slots_ref, send_sem, recv_sem
):
    greeting = greet(chan_places(peers))
    slots_ref[lax.axis_index("chan")] = part_ref[...]
    total, sends = share_and_sum(peers, slots_ref, send_sem, recv_sem, greeting)
    grad = mm(total.astype(BF16), w_ref[...]) + base_ref[...]
    out_ref[...] = mm(order_matrix(out_ref.shape[0], True), grad.astype(BF16)).astype(BF16)
    for copy in sends:
        copy.wait_send()


def shape(dims, dtype=F32):
    return jax.ShapeDtypeStruct(dims, dtype)


def call(kernel, out_shape, scratch, group=None):
    params = dict(vmem_limit_bytes=LIMIT)
    if group is not None:
        params.update(collective_id=group, has_side_effects=True)
    space = pl.BlockSpec(memory_space=pltpu.VMEM)

    def run(*args):
        return pl.pallas_call(
            kernel,
            out_shape=out_shape,
            in_specs=[space] * len(args),
            out_specs=jax.tree.map(lambda _: space, out_shape),
            scratch_shapes=scratch,
            compiler_params=pltpu.CompilerParams(**params),
        )(*args)

    return run


def local(sizes, signal, cotangent, w_proj, w_delta, delta_bias, decay_log, skip_gain):
    rows, width = signal.shape
    depth = decay_log.shape[1]
    steps = rows // SUB
    proj = w_proj.shape[1]
    gates = 4 * depth
    peers = sizes["chan"]
    levels = radices(sizes["seq"])
    vmem = lambda *dims: pltpu.VMEM(dims, F32)
    dma = lambda count: [pltpu.SemaphoreType.DMA((count,))] * 2
    w_turned = w_proj.T
    logs = decay_log.transpose(1, 0, 2)
    slots = [vmem(peers, rows, proj)] + dma(peers - 1)
    projected, sigp, cotp = call(
        functools.partial(project_kernel, peers),
        (shape((rows, proj), BF16), shape((rows, width), BF16), shape((rows, width), BF16)),
        slots,
        0,
    )(signal, cotangent, w_turned)
    common = [
        vmem(2, rows, width),
        vmem(rows, width),
        vmem(rows, width),
        vmem(gates, rows, LANES),
        vmem(2 * depth, SUB, width),
    ]
    pre, entry, span, dev, total = call(
        summary_kernel,
        (
            shape((2, rows, width)),
            shape((2, 2 * depth, SUB, width)),
            shape((2, 2, SUB, width)),
            shape((2, 2 * depth, width), BF16),
            shape((2, width)),
        ),
        common + [vmem(2, 2 * depth, width)],
    )(projected, sigp, cotp, w_delta, delta_bias, logs)
    enter = call(
        functools.partial(exchange_kernel, levels),
        shape((2, 2 * depth, width)),
        [
            [pltpu.VMEM((radix, 2, 2 * depth, width), BF16) for radix in levels],
            [vmem(radix, 2, width) for radix in levels],
            vmem(2 * depth, width),
            vmem(2, 2, width),
        ]
        + dma(2 * sum(radix - 1 for radix in levels)),
        1,
    )(logs, dev, total)
    layer_out, grad_part, base = call(
        scan_kernel,
        (shape((rows, width), BF16), shape((rows, proj)), shape((rows, width))),
        common
        + [
            vmem(rows, width),
            vmem(rows, width),
            vmem(2, rows, width),
            vmem(rows, gates * LANES),
            vmem(steps, depth, SUB, LANES),
            vmem(steps, depth, SUB, LANES),
        ],
    )(
        projected, sigp, cotp, pre, w_delta, logs, skip_gain.reshape(1, width),
        entry, span, enter,
    )
    signal_grad = call(
        functools.partial(final_kernel, peers), shape((rows, width), BF16), slots, 2
    )(grad_part, w_turned, base)
    return (layer_out, signal_grad)


def solution(mesh):
    in_specs = (
        P("seq", "chan"),
        P("seq", "chan"),
        P("chan", None),
        P(None, None, "chan"),
        P(None, "chan"),
        P(None, None, "chan"),
        P("chan"),
    )
    out_specs = (P("seq", "chan"), P("seq", "chan"))
    run = functools.partial(local, dict(mesh.shape))
    return jax.shard_map(run, mesh=mesh, in_specs=in_specs, out_specs=out_specs, check_vma=False)
```

```python
import functools
import math

import jax
import jax.numpy as jnp
from jax import lax
from jax.experimental import pallas as pl
from jax.experimental.pallas import tpu as pltpu
from jax.sharding import PartitionSpec as P

SUB = 8
LANES = 128
MESH = pl.DeviceIdType.MESH
LIMIT = 56 * 1024 * 1024
F32 = jnp.float32
BF16 = jnp.bfloat16
LOG2E = math.log2(math.e)
NT = (((1,), (1,)), ((), ()))


def mm(a, b):
    return jnp.dot(a, b, preferred_element_type=F32)


def order_matrix(rows, back):
    steps = rows // SUB
    work, token = (1, 0) if back else (0, 1)
    r = lax.broadcasted_iota(jnp.int32, (rows, rows), work)
    t = lax.broadcasted_iota(jnp.int32, (rows, rows), token)
    return jnp.where(t == (r & (SUB - 1)) * steps + (r >> 3), 1.0, 0.0).astype(BF16)


def tile_rows(step):
    return pl.ds(pl.multiple_of(step * SUB, SUB), SUB)


def tile_cols(block):
    return pl.ds(pl.multiple_of(block * LANES, LANES), LANES)


def softplus(x):
    return jnp.maximum(x, 0.0) + jnp.log1p(jnp.exp(-jnp.abs(x)))


def fill_rates(log_ref, rate_ref):
    depth = log_ref.shape[0]
    for k in range(2):
        rate = jnp.exp(log_ref[:, k]) * (-LOG2E)
        for n in range(depth):
            rate_ref[k * depth + n] = jnp.broadcast_to(rate[n : n + 1], rate_ref.shape[1:])


def fill_gates(gates, gate_ref):
    for m in range(gate_ref.shape[0]):
        gate_ref[m] = jnp.broadcast_to(gates[:, m : m + 1], gate_ref.shape[1:])


def greet(places):
    barrier = pltpu.get_barrier_semaphore()
    for place in places:
        pl.semaphore_signal(barrier, inc=1, device_id=place, device_id_type=MESH)
    return barrier, len(places)


def share_and_sum(peers, slots_ref, send_sem, recv_sem, greeting):
    me = lax.axis_index("chan")
    pl.semaphore_wait(*greeting)
    sends = []
    for o in range(1, peers):
        copy = pltpu.make_async_remote_copy(
            src_ref=slots_ref.at[me],
            dst_ref=slots_ref.at[me],
            send_sem=send_sem.at[o - 1],
            recv_sem=recv_sem.at[o - 1],
            device_id={"chan": lax.rem(me + o, peers)},
            device_id_type=MESH,
        )
        copy.start()
        sends.append(copy)
    for o in range(1, peers):
        origin = lax.rem(me + peers - o, peers)
        pltpu.make_async_remote_copy(
            src_ref=slots_ref.at[origin],
            dst_ref=slots_ref.at[origin],
            send_sem=send_sem.at[o - 1],
            recv_sem=recv_sem.at[o - 1],
            device_id={"chan": origin},
            device_id_type=MESH,
        ).wait_recv()
    total = slots_ref[0]
    for p in range(1, peers):
        total = total + slots_ref[p]
    return total, sends


def chan_places(peers):
    me = lax.axis_index("chan")
    return [{"chan": lax.rem(me + o, peers)} for o in range(1, peers)]


def project_kernel(
    peers, sig_ref, cot_ref, w_ref, proj_ref, sigp_ref, cotp_ref, slots_ref, send_sem, recv_sem
):
    greeting = greet(chan_places(peers))
    me = lax.axis_index("chan")
    order = order_matrix(sig_ref.shape[0], False)
    sig = mm(order, sig_ref[...]).astype(BF16)
    slots_ref[me] = lax.dot_general(sig, w_ref[...], NT, preferred_element_type=F32)
    sigp_ref[...] = sig
    cotp_ref[...] = mm(order, cot_ref[...]).astype(BF16)
    total, sends = share_and_sum(peers, slots_ref, send_sem, recv_sem, greeting)
    proj_ref[...] = total.astype(BF16)
    for copy in sends:
        copy.wait_send()


def radices(count):
    found = []
    while count % 4 == 0 and count > 4:
        small = count % 16 == 0 and not found
        found += [2, 2] if small else [4]
        count //= 4
    return found + ([count] if count > 1 else [])


def place_at(me, stride, radix, shift):
    digit = lax.rem(me // stride, radix)
    return me + (lax.rem(digit + shift, radix) - digit) * stride


def sublane_scan(decay, value, rising):
    sub = lax.broadcasted_iota(jnp.int32, value.shape, 0)
    shift = 1
    while shift < SUB:
        amount = shift if rising else SUB - shift
        has = (sub >= shift) if rising else (sub < SUB - shift)
        value = value + decay * jnp.where(has, pltpu.roll(value, amount, 0), 0.0)
        decay = decay * jnp.where(has, pltpu.roll(decay, amount, 0), 1.0)
        shift *= 2
    edge = (sub >= 1) if rising else (sub < SUB - 1)
    before = jnp.where(edge, pltpu.roll(value, 1 if rising else SUB - 1, 0), 0.0)
    last = SUB - 1 if rising else 0
    return before, value[last : last + 1]


def core_kernel(
    levels, parts_count, span_lanes,
    proj_ref, sigp_ref, cotp_ref, wd_ref, bias_ref, log_ref, skip_ref,
    out_ref, part_ref, base_ref,
    delta_ref, slope_ref, sig_ref, cot_ref, gate_ref, rate_ref, stack_ref,
    entry_ref, span_ref, edge_ref, total_ref, enter_ref, wide_ref, run_ref,
    core_ref, gsig_ref, gpre_ref, acc_ref, keep_ref, decay_ref,
    part_refs, span_refs, send_sem, recv_sem,
):
    rows, width = sigp_ref.shape
    depth = log_ref.shape[0]
    rank = wd_ref.shape[1]
    steps = rows // SUB
    unroll = math.gcd(steps, 4)
    portion = width // parts_count
    me = lax.axis_index("seq")
    strides = [math.prod(levels[:i]) for i in range(len(levels))]
    greeting = greet(
        [
            {"seq": place_at(me, stride, radix, o)}
            for stride, radix in zip(strides, levels)
            for o in range(1, radix)
        ]
    )
    copies_each = 2 * sum(radix - 1 for radix in levels)
    sends = []

    proj = proj_ref[...]
    for k in range(2):
        pre = mm(proj[:, k * rank : (k + 1) * rank], wd_ref[k]) + bias_ref[k : k + 1, :]
        delta_ref[k] = softplus(pre)
        slope_ref[k] = 1.0 / (1.0 + jnp.exp(-pre))
    sig_ref[...] = sigp_ref[...].astype(F32)
    cot_ref[...] = cotp_ref[...].astype(F32)
    fill_gates(proj[:, 2 * rank :].astype(F32), gate_ref)
    fill_rates(log_ref, rate_ref)
    stack_ref[...] = jnp.exp(jnp.concatenate([log_ref[:, 0], log_ref[:, 1]], 0)) * (-LOG2E)

    def columns(unit):
        return pl.ds(pl.multiple_of(unit * span_lanes, span_lanes), span_lanes)

    def gate(m, here):
        one = gate_ref[m, here, :]
        return jnp.concatenate([one] * (span_lanes // LANES), 1)

    def fold_lanes(value):
        return sum(value[:, i : i + LANES] for i in range(0, span_lanes, LANES))

    def summarize(first_unit, end_unit):
        def unit_body(unit, _):
            cols = columns(unit)
            zero = jnp.zeros((SUB, span_lanes), F32)
            one = jnp.ones((SUB, span_lanes), F32)
            for k in range(2):
                for first in range(0, depth, 4):
                    ns = range(first, min(first + 4, depth))

                    def step_body(i, carry, ns=ns, k=k):
                        span, state, power, adjoint = carry
                        for u in range(unroll):
                            at = i * unroll + u
                            here = tile_rows(at if k == 0 else steps - 1 - at)
                            delta = delta_ref[k, here, cols]
                            weight = delta * sig_ref[here, cols]
                            cot = cot_ref[here, cols]
                            span = span + delta
                            new = ([], [], [])
                            for j, n in enumerate(ns):
                                a = jnp.exp2(delta * rate_ref[k * depth + n, :, cols])
                                p = a * power[j]
                                drive = weight * gate(2 * k * depth + n, here)
                                source = cot * gate((2 * k + 1) * depth + n, here)
                                new[0].append(a * state[j] + drive)
                                new[1].append(p)
                                new[2].append(adjoint[j] + p * source)
                            state, power, adjoint = (tuple(x) for x in new)
                        return span, state, power, adjoint

                    zeros = (zero,) * len(ns)
                    span, state, power, adjoint = lax.fori_loop(
                        0, steps // unroll, step_body, (zero, zeros, (one,) * len(ns), zeros)
                    )
                    if first == 0:
                        below, whole = sublane_scan(one, span, True)
                        above, _unused = sublane_scan(one, span, False)
                        span_ref[0, k, :, cols] = below
                        span_ref[1, k, :, cols] = above
                        total_ref[k : k + 1, cols] = whole
                    for j, n in enumerate(ns):
                        row = k * depth + n
                        for kind, value in ((0, state[j]), (1, adjoint[j])):
                            group = k ^ kind
                            before, edge = sublane_scan(power[j], value, group == 0)
                            entry_ref[group, row, :, cols] = before
                            edge_ref[group, row : row + 1, cols] = edge
            return 0

        if end_unit > first_unit:
            lax.fori_loop(first_unit, end_unit, unit_body, 0)

    def copies(level, q, slot, place, o, group):
        at = q * copies_each + 2 * sum(r - 1 for r in levels[:level]) + 2 * (o - 1)
        parts = part_refs[level].at[q]
        block = parts.at[slot, group] if level == len(levels) - 1 else parts.at[slot]
        return [
            pltpu.make_async_remote_copy(
                src_ref=ref,
                dst_ref=ref,
                send_sem=send_sem.at[at + i],
                recv_sem=recv_sem.at[at + i],
                device_id={"seq": place},
                device_id_type=MESH,
            )
            for i, ref in enumerate((block, span_refs[level].at[q, slot]))
        ]

    def digit_of(level):
        return lax.rem(me // strides[level], levels[level])

    def send(level, q):
        radix, digit = levels[level], digit_of(level)
        if level == 0:
            cols = slice(q * portion, (q + 1) * portion)
            part_refs[0][q, digit] = edge_ref[:, :, cols].astype(BF16)
            span_refs[0][q, digit] = total_ref[:, cols]
        for o in range(1, radix):
            peer = lax.rem(digit + o, radix)
            group = jnp.where(peer > digit, 0, 1)
            place = place_at(me, strides[level], radix, o)
            for copy in copies(level, q, digit, place, o, group):
                copy.start()
                sends.append(copy)

    def settle(level, q):
        radix, digit = levels[level], digit_of(level)
        last = level == len(levels) - 1
        cols = slice(q * portion, (q + 1) * portion)
        for o in range(1, radix):
            peer = lax.rem(digit + radix - o, radix)
            group = jnp.where(peer < digit, 0, 1)
            place = place_at(me, strides[level], radix, radix - o)
            for copy in copies(level, q, peer, place, o, group):
                copy.wait_recv()
        rates = stack_ref[:, cols]
        upper = lax.broadcasted_iota(jnp.int32, rates.shape, 0) < depth
        parts, spans = part_refs[level], span_refs[level]

        def power(span):
            return jnp.exp2(rates * jnp.where(upper, span[0:1], span[1:2]))

        for group in range(2):
            run_ref[...] = jnp.zeros_like(run_ref)
            far = jnp.zeros((2, portion), F32)
            if level == 0:
                enter_ref[group, :, cols] = jnp.zeros(rates.shape, F32)
                wide_ref[q, group] = far
            old = power(wide_ref[q, group])
            for step in range(radix):
                d = step if group == 0 else radix - 1 - step

                @pl.when(digit == d)
                def _(group=group, far=far, old=old):
                    enter_ref[group, :, cols] += old * run_ref[...]
                    wide_ref[q, group] += far

                def advance(d=d, group=group):
                    run_ref[...] = run_ref[...] * power(spans[q, d]) + parts[
                        q, d, group
                    ].astype(F32)

                if last:
                    pl.when((digit > d) if group == 0 else (digit < d))(advance)
                else:
                    advance()
                    far = far + spans[q, d]
            if not last:
                following = digit_of(level + 1)
                part_refs[level + 1][q, following, group] = run_ref[...].astype(BF16)
                if group == 0:
                    span_refs[level + 1][q, following] = far
        if not last:
            send(level + 1, q)

    def start(group, k, n, cols):
        row = k * depth + n
        decay = jnp.exp2(rate_ref[row, :, cols] * span_ref[group, k, :, cols])
        return entry_ref[group, row, :, cols] + decay * enter_ref[group, row : row + 1, cols]

    def gate_lanes(m):
        return slice(m * LANES, (m + 1) * LANES)

    def scan(first_unit, end_unit):
        def unit_body(unit, _):
            cols = columns(unit)
            for k in range(2):
                gate_in = 2 * k * depth
                gate_out = gate_in + depth

                def forward(i, states, k=k, gate_in=gate_in, gate_out=gate_out):
                    for u in range(unroll):
                        at = i * unroll + u
                        at = at if k == 0 else steps - 1 - at
                        here = tile_rows(at)
                        delta = delta_ref[k, here, cols]
                        weight = delta * sig_ref[here, cols]
                        cot = cot_ref[here, cols]
                        total = jnp.zeros((SUB, span_lanes), F32)
                        new = []
                        for n in range(depth):
                            a = jnp.exp2(delta * rate_ref[k * depth + n, :, cols])
                            kept = a * states[n]
                            h = kept + weight * gate(gate_in + n, here)
                            decay_ref[at, n] = a
                            keep_ref[at, n] = kept
                            total = total + gate(gate_out + n, here) * h
                            acc_ref[here, gate_lanes(gate_out + n)] += fold_lanes(cot * h)
                            new.append(h)
                        if k == 0:
                            core_ref[here, cols] = total
                        else:
                            core_ref[here, cols] += total
                        states = tuple(new)
                    return states

                lax.fori_loop(
                    0, steps // unroll, forward, tuple(start(k, k, n, cols) for n in range(depth))
                )

                def backward(i, carried, k=k, gate_in=gate_in, gate_out=gate_out):
                    for u in range(unroll):
                        at = i * unroll + u
                        at = steps - 1 - at if k == 0 else at
                        here = tile_rows(at)
                        delta = delta_ref[k, here, cols]
                        sig = sig_ref[here, cols]
                        weight = delta * sig
                        cot = cot_ref[here, cols]
                        by_in = jnp.zeros((SUB, span_lanes), F32)
                        by_decay = jnp.zeros((SUB, span_lanes), F32)
                        new = []
                        for n in range(depth):
                            adjoint = cot * gate(gate_out + n, here) + carried[n]
                            by_in = by_in + adjoint * gate(gate_in + n, here)
                            by_decay = by_decay + adjoint * (
                                keep_ref[at, n] * rate_ref[k * depth + n, :, cols]
                            )
                            acc_ref[here, gate_lanes(gate_in + n)] += fold_lanes(adjoint * weight)
                            new.append(decay_ref[at, n] * adjoint)
                        if k == 0:
                            gsig_ref[here, cols] = by_in * delta
                        else:
                            gsig_ref[here, cols] += by_in * delta
                        gpre_ref[k, here, cols] = by_in * sig + by_decay * (1.0 / LOG2E)
                        carried = tuple(new)
                    return carried

                lax.fori_loop(
                    0,
                    steps // unroll,
                    backward,
                    tuple(start(1 - k, k, n, cols) for n in range(depth)),
                )
            return 0

        if end_unit > first_unit:
            lax.fori_loop(first_unit, end_unit, unit_body, 0)

    half = portion // span_lanes
    mid = half // 2
    top = len(levels)
    summarize(0, half)
    pl.semaphore_wait(*greeting)
    send(0, 0)
    summarize(half, half + mid)
    settle(0, 0)
    summarize(half + mid, 2 * half)
    send(0, 1)
    acc_ref[...] = jnp.zeros_like(acc_ref)
    for level in range(1, top - 1):
        settle(level, 0)
    settle(0, 1)
    settle(top - 1, 0)
    scan(0, mid)
    for level in range(1, top - 1):
        settle(level, 1)
    scan(mid, half)
    settle(top - 1, 1)
    scan(half, 2 * half)

    skip = skip_ref[...]
    layer = (core_ref[...] + skip * sig_ref[...]).astype(BF16)
    out_ref[...] = mm(order_matrix(rows, True), layer).astype(BF16)
    base_ref[...] = gsig_ref[...] + skip * cot_ref[...]
    for k in range(2):
        grad_pre = (gpre_ref[k] * slope_ref[k]).astype(BF16)
        part_ref[:, k * rank : (k + 1) * rank] = lax.dot_general(
            grad_pre, wd_ref[k], NT, preferred_element_type=F32
        )
    gates = 4 * depth
    acc = acc_ref[...]
    high = acc.astype(BF16)
    low = (acc - high.astype(F32)).astype(BF16)
    lane = lax.broadcasted_iota(jnp.int32, (gates * LANES, gates), 0) >> 7
    column = lax.broadcasted_iota(jnp.int32, (gates * LANES, gates), 1)
    ones = jnp.where(lane == column, 1.0, 0.0).astype(BF16)
    part_ref[:, 2 * rank :] = mm(high, ones) + mm(low, ones)
    for copy in sends:
        copy.wait_send()


def final_kernel(
    peers, part_ref, w_ref, base_ref, out_ref, slots_ref, send_sem, recv_sem
):
    greeting = greet(chan_places(peers))
    slots_ref[lax.axis_index("chan")] = part_ref[...]
    total, sends = share_and_sum(peers, slots_ref, send_sem, recv_sem, greeting)
    grad = mm(total.astype(BF16), w_ref[...]) + base_ref[...]
    out_ref[...] = mm(order_matrix(out_ref.shape[0], True), grad.astype(BF16)).astype(BF16)
    for copy in sends:
        copy.wait_send()


def shape(dims, dtype=F32):
    return jax.ShapeDtypeStruct(dims, dtype)


def call(kernel, out_shape, scratch, group=None):
    params = dict(vmem_limit_bytes=LIMIT)
    if group is not None:
        params.update(collective_id=group, has_side_effects=True)
    space = pl.BlockSpec(memory_space=pltpu.VMEM)

    def run(*args):
        return pl.pallas_call(
            kernel,
            out_shape=out_shape,
            in_specs=[space] * len(args),
            out_specs=jax.tree.map(lambda _: space, out_shape),
            scratch_shapes=scratch,
            compiler_params=pltpu.CompilerParams(**params),
        )(*args)

    return run


def local(sizes, signal, cotangent, w_proj, w_delta, delta_bias, decay_log, skip_gain):
    rows, width = signal.shape
    depth = decay_log.shape[1]
    steps = rows // SUB
    proj = w_proj.shape[1]
    gates = 4 * depth
    peers = sizes["chan"]
    levels = radices(sizes["seq"])
    vmem = lambda *dims: pltpu.VMEM(dims, F32)
    dma = lambda count: [pltpu.SemaphoreType.DMA((count,))] * 2
    w_turned = w_proj.T
    logs = decay_log.transpose(1, 0, 2)
    slots = [vmem(peers, rows, proj)] + dma(peers - 1)
    projected, sigp, cotp = call(
        functools.partial(project_kernel, peers),
        (shape((rows, proj), BF16), shape((rows, width), BF16), shape((rows, width), BF16)),
        slots,
        0,
    )(signal, cotangent, w_turned)
    parts_count = 2
    portion = width // parts_count
    span_lanes = math.gcd(portion, 2 * LANES)
    layer_out, grad_part, base = call(
        functools.partial(core_kernel, levels, parts_count, span_lanes),
        (shape((rows, width), BF16), shape((rows, proj)), shape((rows, width))),
        [
            vmem(2, rows, width),
            vmem(2, rows, width),
            vmem(rows, width),
            vmem(rows, width),
            vmem(gates, rows, LANES),
            vmem(2 * depth, SUB, width),
            vmem(2 * depth, width),
            vmem(2, 2 * depth, SUB, width),
            vmem(2, 2, SUB, width),
            vmem(2, 2 * depth, width),
            vmem(2, width),
            vmem(2, 2 * depth, width),
            vmem(parts_count, 2, 2, portion),
            vmem(2 * depth, portion),
            vmem(rows, width),
            vmem(rows, width),
            vmem(2, rows, width),
            vmem(rows, gates * LANES),
            vmem(steps, depth, SUB, span_lanes),
            vmem(steps, depth, SUB, span_lanes),
            [pltpu.VMEM((parts_count, r, 2, 2 * depth, portion), BF16) for r in levels],
            [vmem(parts_count, r, 2, portion) for r in levels],
        ]
        + dma(parts_count * 2 * sum(r - 1 for r in levels)),
        1,
    )(projected, sigp, cotp, w_delta, delta_bias, logs, skip_gain.reshape(1, width))
    signal_grad = call(
        functools.partial(final_kernel, peers), shape((rows, width), BF16), slots, 2
    )(grad_part, w_turned, base)
    return (layer_out, signal_grad)


def solution(mesh):
    in_specs = (
        P("seq", "chan"),
        P("seq", "chan"),
        P("chan", None),
        P(None, None, "chan"),
        P(None, "chan"),
        P(None, None, "chan"),
        P("chan"),
    )
    out_specs = (P("seq", "chan"), P("seq", "chan"))
    run = functools.partial(local, dict(mesh.shape))
    return jax.shard_map(run, mesh=mesh, in_specs=in_specs, out_specs=out_specs, check_vma=False)
```

```python
import functools
import math

import jax
import jax.numpy as jnp
from jax import lax
from jax.experimental import pallas as pl
from jax.experimental.pallas import tpu as pltpu
from jax.sharding import PartitionSpec as P

SUB = 8
LANES = 128
MESH = pl.DeviceIdType.MESH
LIMIT = 56 * 1024 * 1024
F32 = jnp.float32
BF16 = jnp.bfloat16
LOG2E = math.log2(math.e)
NT = (((1,), (1,)), ((), ()))


def mm(a, b):
    return jnp.dot(a, b, preferred_element_type=F32)


def order_matrix(rows, back):
    steps = rows // SUB
    work, token = (1, 0) if back else (0, 1)
    r = lax.broadcasted_iota(jnp.int32, (rows, rows), work)
    t = lax.broadcasted_iota(jnp.int32, (rows, rows), token)
    return jnp.where(t == (r & (SUB - 1)) * steps + (r >> 3), 1.0, 0.0).astype(BF16)


def tile_rows(step):
    return pl.ds(pl.multiple_of(step * SUB, SUB), SUB)


def tile_cols(block):
    return pl.ds(pl.multiple_of(block * LANES, LANES), LANES)


def softplus(x):
    return jnp.maximum(x, 0.0) + jnp.log1p(jnp.exp(-jnp.abs(x)))


def fill_rates(log_ref, rate_ref):
    depth = log_ref.shape[0]
    for k in range(2):
        rate = jnp.exp(log_ref[:, k]) * (-LOG2E)
        for n in range(depth):
            rate_ref[k * depth + n] = jnp.broadcast_to(rate[n : n + 1], rate_ref.shape[1:])


def fill_gates(gates, gate_ref):
    for m in range(gate_ref.shape[0]):
        gate_ref[m] = jnp.broadcast_to(gates[:, m : m + 1], gate_ref.shape[1:])


def greet(places):
    barrier = pltpu.get_barrier_semaphore()
    for place in places:
        pl.semaphore_signal(barrier, inc=1, device_id=place, device_id_type=MESH)
    return barrier, len(places)


def share_and_sum(peers, slots_ref, send_sem, recv_sem, greeting):
    me = lax.axis_index("chan")
    pl.semaphore_wait(*greeting)
    sends = []
    for o in range(1, peers):
        copy = pltpu.make_async_remote_copy(
            src_ref=slots_ref.at[me],
            dst_ref=slots_ref.at[me],
            send_sem=send_sem.at[o - 1],
            recv_sem=recv_sem.at[o - 1],
            device_id={"chan": lax.rem(me + o, peers)},
            device_id_type=MESH,
        )
        copy.start()
        sends.append(copy)
    for o in range(1, peers):
        origin = lax.rem(me + peers - o, peers)
        pltpu.make_async_remote_copy(
            src_ref=slots_ref.at[origin],
            dst_ref=slots_ref.at[origin],
            send_sem=send_sem.at[o - 1],
            recv_sem=recv_sem.at[o - 1],
            device_id={"chan": origin},
            device_id_type=MESH,
        ).wait_recv()
    total = slots_ref[0]
    for p in range(1, peers):
        total = total + slots_ref[p]
    return total, sends


def chan_places(peers):
    me = lax.axis_index("chan")
    return [{"chan": lax.rem(me + o, peers)} for o in range(1, peers)]


def project_kernel(
    peers, sig_ref, cot_ref, w_ref, proj_ref, sigp_ref, cotp_ref, slots_ref, send_sem, recv_sem
):
    greeting = greet(chan_places(peers))
    me = lax.axis_index("chan")
    order = order_matrix(sig_ref.shape[0], False)
    sig = mm(order, sig_ref[...]).astype(BF16)
    slots_ref[me] = lax.dot_general(sig, w_ref[...], NT, preferred_element_type=F32)
    sigp_ref[...] = sig
    cotp_ref[...] = mm(order, cot_ref[...]).astype(BF16)
    total, sends = share_and_sum(peers, slots_ref, send_sem, recv_sem, greeting)
    proj_ref[...] = total.astype(BF16)
    for copy in sends:
        copy.wait_send()


def radices(count):
    found = []
    while count % 4 == 0 and count > 4:
        small = count % 16 == 0 and not found
        found += [2, 2] if small else [4]
        count //= 4
    return found + ([count] if count > 1 else [])


def place_at(me, stride, radix, shift):
    digit = lax.rem(me // stride, radix)
    return me + (lax.rem(digit + shift, radix) - digit) * stride


def sublane_scan(decay, value, rising):
    sub = lax.broadcasted_iota(jnp.int32, value.shape, 0)
    shift = 1
    while shift < SUB:
        amount = shift if rising else SUB - shift
        has = (sub >= shift) if rising else (sub < SUB - shift)
        value = value + decay * jnp.where(has, pltpu.roll(value, amount, 0), 0.0)
        decay = decay * jnp.where(has, pltpu.roll(decay, amount, 0), 1.0)
        shift *= 2
    edge = (sub >= 1) if rising else (sub < SUB - 1)
    before = jnp.where(edge, pltpu.roll(value, 1 if rising else SUB - 1, 0), 0.0)
    last = SUB - 1 if rising else 0
    return before, value[last : last + 1]


def core_kernel(
    levels, parts_count, span_lanes,
    proj_ref, sigp_ref, cotp_ref, wd_ref, bias_ref, log_ref, skip_ref,
    out_ref, part_ref, base_ref,
    delta_ref, slope_ref, sig_ref, cot_ref, gate_ref, rate_ref, stack_ref,
    entry_ref, span_ref, edge_ref, total_ref, enter_ref, wide_ref, run_ref,
    core_ref, gsig_ref, gpre_ref, acc_ref, keep_ref, decay_ref,
    part_refs, span_refs, send_sem, recv_sem,
):
    rows, width = sigp_ref.shape
    depth = log_ref.shape[0]
    rank = wd_ref.shape[1]
    steps = rows // SUB
    unroll = math.gcd(steps, 8)
    portion = width // parts_count
    me = lax.axis_index("seq")
    strides = [math.prod(levels[:i]) for i in range(len(levels))]
    greeting = greet(
        [
            {"seq": place_at(me, stride, radix, o)}
            for stride, radix in zip(strides, levels)
            for o in range(1, radix)
        ]
    )
    copies_each = 2 * sum(radix - 1 for radix in levels)
    sends = []

    proj = proj_ref[...]
    for k in range(2):
        pre = mm(proj[:, k * rank : (k + 1) * rank], wd_ref[k]) + bias_ref[k : k + 1, :]
        delta_ref[k] = softplus(pre)
        slope_ref[k] = 1.0 / (1.0 + jnp.exp(-pre))
    sig_ref[...] = sigp_ref[...].astype(F32)
    cot_ref[...] = cotp_ref[...].astype(F32)
    fill_gates(proj[:, 2 * rank :].astype(F32), gate_ref)
    fill_rates(log_ref, rate_ref)
    stack_ref[...] = jnp.exp(jnp.concatenate([log_ref[:, 0], log_ref[:, 1]], 0)) * (-LOG2E)

    def columns(unit):
        return pl.ds(pl.multiple_of(unit * span_lanes, span_lanes), span_lanes)

    def gate(m, here):
        one = gate_ref[m, here, :]
        return jnp.concatenate([one] * (span_lanes // LANES), 1)

    def fold_lanes(value):
        return sum(value[:, i : i + LANES] for i in range(0, span_lanes, LANES))

    def summarize(first_unit, end_unit):
        def unit_body(unit, _):
            cols = columns(unit)
            zero = jnp.zeros((SUB, span_lanes), F32)
            one = jnp.ones((SUB, span_lanes), F32)
            for k in range(2):
                for first in range(0, depth, 4):
                    ns = range(first, min(first + 4, depth))

                    def step_body(i, carry, ns=ns, k=k):
                        span, state, power, adjoint = carry
                        for u in range(unroll):
                            at = i * unroll + u
                            here = tile_rows(at if k == 0 else steps - 1 - at)
                            delta = delta_ref[k, here, cols]
                            weight = delta * sig_ref[here, cols]
                            cot = cot_ref[here, cols]
                            span = span + delta
                            new = ([], [], [])
                            for j, n in enumerate(ns):
                                a = jnp.exp2(delta * rate_ref[k * depth + n, :, cols])
                                p = a * power[j]
                                drive = weight * gate(2 * k * depth + n, here)
                                source = cot * gate((2 * k + 1) * depth + n, here)
                                new[0].append(a * state[j] + drive)
                                new[1].append(p)
                                new[2].append(adjoint[j] + p * source)
                            state, power, adjoint = (tuple(x) for x in new)
                        return span, state, power, adjoint

                    zeros = (zero,) * len(ns)
                    span, state, power, adjoint = lax.fori_loop(
                        0, steps // unroll, step_body, (zero, zeros, (one,) * len(ns), zeros)
                    )
                    if first == 0:
                        below, whole = sublane_scan(one, span, True)
                        above, _unused = sublane_scan(one, span, False)
                        span_ref[0, k, :, cols] = below
                        span_ref[1, k, :, cols] = above
                        total_ref[k : k + 1, cols] = whole
                    for j, n in enumerate(ns):
                        row = k * depth + n
                        for kind, value in ((0, state[j]), (1, adjoint[j])):
                            group = k ^ kind
                            before, edge = sublane_scan(power[j], value, group == 0)
                            entry_ref[group, row, :, cols] = before
                            edge_ref[group, row : row + 1, cols] = edge
            return 0

        if end_unit > first_unit:
            lax.fori_loop(first_unit, end_unit, unit_body, 0)

    def copies(level, q, slot, place, o, group):
        at = q * copies_each + 2 * sum(r - 1 for r in levels[:level]) + 2 * (o - 1)
        parts = part_refs[level].at[q]
        block = parts.at[slot, group] if level == len(levels) - 1 else parts.at[slot]
        return [
            pltpu.make_async_remote_copy(
                src_ref=ref,
                dst_ref=ref,
                send_sem=send_sem.at[at + i],
                recv_sem=recv_sem.at[at + i],
                device_id={"seq": place},
                device_id_type=MESH,
            )
            for i, ref in enumerate((block, span_refs[level].at[q, slot]))
        ]

    def digit_of(level):
        return lax.rem(me // strides[level], levels[level])

    def send(level, q):
        radix, digit = levels[level], digit_of(level)
        if level == 0:
            cols = slice(q * portion, (q + 1) * portion)
            part_refs[0][q, digit] = edge_ref[:, :, cols].astype(BF16)
            span_refs[0][q, digit] = total_ref[:, cols]
        for o in range(1, radix):
            peer = lax.rem(digit + o, radix)
            group = jnp.where(peer > digit, 0, 1)
            place = place_at(me, strides[level], radix, o)
            for copy in copies(level, q, digit, place, o, group):
                copy.start()
                sends.append(copy)

    def settle(level, q):
        radix, digit = levels[level], digit_of(level)
        last = level == len(levels) - 1
        cols = slice(q * portion, (q + 1) * portion)
        for o in range(1, radix):
            peer = lax.rem(digit + radix - o, radix)
            group = jnp.where(peer < digit, 0, 1)
            place = place_at(me, strides[level], radix, radix - o)
            for copy in copies(level, q, peer, place, o, group):
                copy.wait_recv()
        rates = stack_ref[:, cols]
        upper = lax.broadcasted_iota(jnp.int32, rates.shape, 0) < depth
        parts, spans = part_refs[level], span_refs[level]

        def power(span):
            return jnp.exp2(rates * jnp.where(upper, span[0:1], span[1:2]))

        for group in range(2):
            run_ref[...] = jnp.zeros_like(run_ref)
            far = jnp.zeros((2, portion), F32)
            if level == 0:
                enter_ref[group, :, cols] = jnp.zeros(rates.shape, F32)
                wide_ref[q, group] = far
            old = power(wide_ref[q, group])
            for step in range(radix):
                d = step if group == 0 else radix - 1 - step

                @pl.when(digit == d)
                def _(group=group, far=far, old=old):
                    enter_ref[group, :, cols] += old * run_ref[...]
                    wide_ref[q, group] += far

                def advance(d=d, group=group):
                    run_ref[...] = run_ref[...] * power(spans[q, d]) + parts[
                        q, d, group
                    ].astype(F32)

                if last:
                    pl.when((digit > d) if group == 0 else (digit < d))(advance)
                else:
                    advance()
                    far = far + spans[q, d]
            if not last:
                following = digit_of(level + 1)
                part_refs[level + 1][q, following, group] = run_ref[...].astype(BF16)
                if group == 0:
                    span_refs[level + 1][q, following] = far
        if not last:
            send(level + 1, q)

    def start(group, k, n, cols):
        row = k * depth + n
        decay = jnp.exp2(rate_ref[row, :, cols] * span_ref[group, k, :, cols])
        return entry_ref[group, row, :, cols] + decay * enter_ref[group, row : row + 1, cols]

    def gate_lanes(m):
        return slice(m * LANES, (m + 1) * LANES)

    def scan(first_unit, end_unit):
        def unit_body(unit, _):
            cols = columns(unit)
            for k in range(2):
                gate_in = 2 * k * depth
                gate_out = gate_in + depth

                def forward(i, states, k=k, gate_in=gate_in, gate_out=gate_out):
                    for u in range(unroll):
                        at = i * unroll + u
                        at = at if k == 0 else steps - 1 - at
                        here = tile_rows(at)
                        delta = delta_ref[k, here, cols]
                        weight = delta * sig_ref[here, cols]
                        cot = cot_ref[here, cols]
                        total = jnp.zeros((SUB, span_lanes), F32)
                        new = []
                        for n in range(depth):
                            a = jnp.exp2(delta * rate_ref[k * depth + n, :, cols])
                            kept = a * states[n]
                            h = kept + weight * gate(gate_in + n, here)
                            decay_ref[at, n] = a
                            keep_ref[at, n] = kept
                            total = total + gate(gate_out + n, here) * h
                            acc_ref[here, gate_lanes(gate_out + n)] += fold_lanes(cot * h)
                            new.append(h)
                        if k == 0:
                            core_ref[here, cols] = total
                        else:
                            core_ref[here, cols] += total
                        states = tuple(new)
                    return states

                lax.fori_loop(
                    0, steps // unroll, forward, tuple(start(k, k, n, cols) for n in range(depth))
                )

                def backward(i, carried, k=k, gate_in=gate_in, gate_out=gate_out):
                    for u in range(unroll):
                        at = i * unroll + u
                        at = steps - 1 - at if k == 0 else at
                        here = tile_rows(at)
                        delta = delta_ref[k, here, cols]
                        sig = sig_ref[here, cols]
                        weight = delta * sig
                        cot = cot_ref[here, cols]
                        by_in = jnp.zeros((SUB, span_lanes), F32)
                        by_decay = jnp.zeros((SUB, span_lanes), F32)
                        new = []
                        for n in range(depth):
                            adjoint = cot * gate(gate_out + n, here) + carried[n]
                            by_in = by_in + adjoint * gate(gate_in + n, here)
                            by_decay = by_decay + adjoint * (
                                keep_ref[at, n] * rate_ref[k * depth + n, :, cols]
                            )
                            acc_ref[here, gate_lanes(gate_in + n)] += fold_lanes(adjoint * weight)
                            new.append(decay_ref[at, n] * adjoint)
                        if k == 0:
                            gsig_ref[here, cols] = by_in * delta
                        else:
                            gsig_ref[here, cols] += by_in * delta
                        gpre_ref[k, here, cols] = by_in * sig + by_decay * (1.0 / LOG2E)
                        carried = tuple(new)
                    return carried

                lax.fori_loop(
                    0,
                    steps // unroll,
                    backward,
                    tuple(start(1 - k, k, n, cols) for n in range(depth)),
                )
            return 0

        if end_unit > first_unit:
            lax.fori_loop(first_unit, end_unit, unit_body, 0)

    half = portion // span_lanes
    mid = half // 2
    top = len(levels)
    summarize(0, half)
    pl.semaphore_wait(*greeting)
    send(0, 0)
    summarize(half, half + mid)
    settle(0, 0)
    summarize(half + mid, 2 * half)
    send(0, 1)
    acc_ref[...] = jnp.zeros_like(acc_ref)
    for level in range(1, top - 1):
        settle(level, 0)
    settle(0, 1)
    settle(top - 1, 0)
    scan(0, mid)
    for level in range(1, top - 1):
        settle(level, 1)
    scan(mid, half)
    settle(top - 1, 1)
    scan(half, 2 * half)

    skip = skip_ref[...]
    layer = (core_ref[...] + skip * sig_ref[...]).astype(BF16)
    out_ref[...] = mm(order_matrix(rows, True), layer).astype(BF16)
    base_ref[...] = gsig_ref[...] + skip * cot_ref[...]
    for k in range(2):
        grad_pre = (gpre_ref[k] * slope_ref[k]).astype(BF16)
        part_ref[:, k * rank : (k + 1) * rank] = lax.dot_general(
            grad_pre, wd_ref[k], NT, preferred_element_type=F32
        )
    gates = 4 * depth
    acc = acc_ref[...]
    high = acc.astype(BF16)
    low = (acc - high.astype(F32)).astype(BF16)
    lane = lax.broadcasted_iota(jnp.int32, (gates * LANES, gates), 0) >> 7
    column = lax.broadcasted_iota(jnp.int32, (gates * LANES, gates), 1)
    ones = jnp.where(lane == column, 1.0, 0.0).astype(BF16)
    part_ref[:, 2 * rank :] = mm(high, ones) + mm(low, ones)
    for copy in sends:
        copy.wait_send()


def final_kernel(
    peers, part_ref, w_ref, base_ref, out_ref, slots_ref, send_sem, recv_sem
):
    greeting = greet(chan_places(peers))
    slots_ref[lax.axis_index("chan")] = part_ref[...]
    total, sends = share_and_sum(peers, slots_ref, send_sem, recv_sem, greeting)
    grad = mm(total.astype(BF16), w_ref[...]) + base_ref[...]
    out_ref[...] = mm(order_matrix(out_ref.shape[0], True), grad.astype(BF16)).astype(BF16)
    for copy in sends:
        copy.wait_send()


def shape(dims, dtype=F32):
    return jax.ShapeDtypeStruct(dims, dtype)


def call(kernel, out_shape, scratch, group=None):
    params = dict(vmem_limit_bytes=LIMIT)
    if group is not None:
        params.update(collective_id=group, has_side_effects=True)
    space = pl.BlockSpec(memory_space=pltpu.VMEM)

    def run(*args):
        return pl.pallas_call(
            kernel,
            out_shape=out_shape,
            in_specs=[space] * len(args),
            out_specs=jax.tree.map(lambda _: space, out_shape),
            scratch_shapes=scratch,
            compiler_params=pltpu.CompilerParams(**params),
        )(*args)

    return run


def local(sizes, signal, cotangent, w_proj, w_delta, delta_bias, decay_log, skip_gain):
    rows, width = signal.shape
    depth = decay_log.shape[1]
    steps = rows // SUB
    proj = w_proj.shape[1]
    gates = 4 * depth
    peers = sizes["chan"]
    levels = radices(sizes["seq"])
    vmem = lambda *dims: pltpu.VMEM(dims, F32)
    dma = lambda count: [pltpu.SemaphoreType.DMA((count,))] * 2
    w_turned = w_proj.T
    logs = decay_log.transpose(1, 0, 2)
    slots = [vmem(peers, rows, proj)] + dma(peers - 1)
    projected, sigp, cotp = call(
        functools.partial(project_kernel, peers),
        (shape((rows, proj), BF16), shape((rows, width), BF16), shape((rows, width), BF16)),
        slots,
        0,
    )(signal, cotangent, w_turned)
    parts_count = 2
    portion = width // parts_count
    span_lanes = math.gcd(portion, 2 * LANES)
    layer_out, grad_part, base = call(
        functools.partial(core_kernel, levels, parts_count, span_lanes),
        (shape((rows, width), BF16), shape((rows, proj)), shape((rows, width))),
        [
            vmem(2, rows, width),
            vmem(2, rows, width),
            vmem(rows, width),
            vmem(rows, width),
            vmem(gates, rows, LANES),
            vmem(2 * depth, SUB, width),
            vmem(2 * depth, width),
            vmem(2, 2 * depth, SUB, width),
            vmem(2, 2, SUB, width),
            vmem(2, 2 * depth, width),
            vmem(2, width),
            vmem(2, 2 * depth, width),
            vmem(parts_count, 2, 2, portion),
            vmem(2 * depth, portion),
            vmem(rows, width),
            vmem(rows, width),
            vmem(2, rows, width),
            vmem(rows, gates * LANES),
            vmem(steps, depth, SUB, span_lanes),
            vmem(steps, depth, SUB, span_lanes),
            [pltpu.VMEM((parts_count, r, 2, 2 * depth, portion), BF16) for r in levels],
            [vmem(parts_count, r, 2, portion) for r in levels],
        ]
        + dma(parts_count * 2 * sum(r - 1 for r in levels)),
        1,
    )(projected, sigp, cotp, w_delta, delta_bias, logs, skip_gain.reshape(1, width))
    signal_grad = call(
        functools.partial(final_kernel, peers), shape((rows, width), BF16), slots, 2
    )(grad_part, w_turned, base)
    return (layer_out, signal_grad)


def solution(mesh):
    in_specs = (
        P("seq", "chan"),
        P("seq", "chan"),
        P("chan", None),
        P(None, None, "chan"),
        P(None, "chan"),
        P(None, None, "chan"),
        P("chan"),
    )
    out_specs = (P("seq", "chan"), P("seq", "chan"))
    run = functools.partial(local, dict(mesh.shape))
    return jax.shard_map(run, mesh=mesh, in_specs=in_specs, out_specs=out_specs, check_vma=False)
```
